32 devices in a mesh: row: 8 (over z, core), col: 4 (over y, x).
Axes of the slice: x: 2, y: 2, z: 4, core: 2. Of those that a mesh axis runs over, the one named last changes fastest.
Arguments:
- trailing: float32 [4, 8, 512, 8, 4, 512], P(None, 'row', None, None, 'col'), as said below
Outputs:
- factor: float32 [4, 8, 512, 8, 4, 512], P(None, 'row', None, None, 'col')
Inputs may be any that keep to these rules, and one draw needn't show every extreme that they name: trailing is symmetric and positive definite, with entries of at least 0.
All inputs are finite; a program needn't handle non-finite values.
Results may differ from the reference program's by a relative error of at most 0.0003.
Values sent between devices are 32-bit elements; how exact they have to be, the bound alone decides.
A program may use at most 192 MiB of HBM per device.

```python
import math
import jax
import jax.numpy as jnp
from jax import lax

B = 512
IB = 128
TILES = 32
STEPS = 2
GX = 128
ROW_TILES = 4
COL_TILES = 8


SQRT_THREE = math.sqrt(3.0)


NUGGET_VALUE = 0.5


def draw_trailing(key, part):
    order_rows = TILES * B
    shuffled = jax.random.permutation(jax.random.fold_in(key, 7), order_rows)
    first_coord = (shuffled % GX).astype(jnp.float32)
    second_coord = (shuffled // GX).astype(jnp.float32)
    length = 20.0
    all_columns = jnp.arange(order_rows, dtype=jnp.int32)

    def tile_row(row_start):
        rows_first = lax.dynamic_slice_in_dim(first_coord, row_start, B)
        rows_second = lax.dynamic_slice_in_dim(second_coord, row_start, B)
        rows_number = row_start + jnp.arange(B, dtype=jnp.int32)
        delta_first = rows_first[:, None] - first_coord[None, :]
        delta_second = rows_second[:, None] - second_coord[None, :]
        distance = jnp.sqrt(delta_first * delta_first + delta_second * delta_second)
        scaled = SQRT_THREE * distance / length
        covariance = (1.0 + scaled) * jnp.exp(-scaled)
        nugget_part = jnp.where(rows_number[:, None] == all_columns[None, :], NUGGET_VALUE, 0.0)
        return covariance + nugget_part
    full = lax.map(tile_row, jnp.arange(TILES, dtype=jnp.int32) * B)
    return full.reshape(ROW_TILES, TILES // ROW_TILES, B, COL_TILES, TILES // COL_TILES, B).astype(jnp.float32)


def setup_inputs(seed: int = 0) -> dict:
    key_of = jax.random.split(jax.random.key(seed), 2)
    trailing = draw_trailing(jax.random.fold_in(key_of[1], 71), 0)
    return dict(trailing=trailing)


def tri_inverse(lower_tri, block_size):
    block_count = lower_tri.shape[0] // block_size
    identity = jnp.eye(block_size, dtype=lower_tri.dtype)

    def piece_of(p, q):
        return lower_tri[p * block_size:(p + 1) * block_size, q * block_size:(q + 1) * block_size]
    inverse = [[jnp.zeros((block_size, block_size), lower_tri.dtype) for q in range(block_count)] for p in range(block_count)]
    for p in range(block_count):
        inverse[p][p] = lax.linalg.triangular_solve(piece_of(p, p), identity, left_side=True, lower=True)
    for p in range(block_count):
        for q in range(p):
            partial_sum = jnp.zeros((block_size, block_size), lower_tri.dtype)
            for s in range(q, p):
                partial_sum = partial_sum + jnp.dot(piece_of(p, s), inverse[s][q], precision=lax.Precision.HIGHEST)
            inverse[p][q] = -jnp.dot(inverse[p][p], partial_sum, precision=lax.Precision.HIGHEST)
    return jnp.block(inverse)

def reference(trailing):
    tile_count = trailing.shape[0] * trailing.shape[1]
    tile_size = trailing.shape[2]
    full = trailing.reshape(tile_count, tile_size, tile_count, tile_size)
    tile_index = jnp.arange(tile_count, dtype=jnp.int32)
    for k in range(STEPS):
        factor_kk = jnp.linalg.cholesky(full[k, :, k, :])
        panel_tiles = jnp.einsum('iab,cb->iac', full[:, :, k, :], tri_inverse(factor_kk, IB), precision=lax.Precision.HIGHEST)
        live_rows = (tile_index > k)[:, None, None]
        panel_tiles = jnp.where(live_rows, panel_tiles, 0.0)
        new_column = jnp.where(live_rows, panel_tiles, jnp.where((tile_index == k)[:, None, None], jnp.tril(factor_kk)[None], full[:, :, k, :]))
        full = full.at[:, :, k, :].set(new_column)

        def update_row(row_item, panel_tiles=panel_tiles, k=k):
            row_block, row_panel, row_number = row_item
            product = jnp.einsum('ab,jcb->ajc', row_panel, panel_tiles, precision=lax.Precision.HIGHEST)
            allowed = (tile_index <= row_number) & (tile_index > k)
            return row_block - jnp.where(allowed[None, :, None], product, 0.0)
        full = lax.map(update_row, (full, panel_tiles, tile_index))
    keep_tiles = tile_index[:, None, None, None] >= tile_index[None, None, :, None]
    return jnp.where(keep_tiles, full, 0.0).reshape(trailing.shape)
```

```python
import functools

import jax
import jax.numpy as jnp
from jax import lax
from jax.experimental import pallas as pl
from jax.experimental.pallas import tpu as pltpu
from jax.sharding import PartitionSpec as P

IB = 128
STEPS = 2
HIGHEST = lax.Precision.HIGHEST


def eliminate(block):
    n = IB
    groups = n // 8
    rows = [block[8 * g : 8 * g + 8, :] for g in range(groups)]
    lane = lax.broadcasted_iota(jnp.int32, (1, n), 1)
    sub = lax.broadcasted_iota(jnp.int32, (8, 1), 0)
    for j in range(n):
        g0, jj = j // 8, j % 8
        row = rows[g0][jj : jj + 1, :]
        inv = 1.0 / row[:, j : j + 1]
        here = lane == j
        pivot_row = jnp.where(here, 1.0, row)
        for g in range(g0, groups):
            if g == g0 and jj == 7:
                continue
            factor = rows[g][:, j : j + 1] * inv
            if g == g0:
                below = sub > jj
                factor = jnp.where(below, factor, 0.0)
                base = jnp.where(here & below, 0.0, rows[g])
            else:
                base = jnp.where(here, 0.0, rows[g])
            rows[g] = base - factor * pivot_row
    full = jnp.concatenate(rows, axis=0)
    r = lax.broadcasted_iota(jnp.int32, (n, n), 0)
    c = lax.broadcasted_iota(jnp.int32, (n, n), 1)
    diag = jnp.sum(jnp.where(r == c, full, 0.0), axis=1, keepdims=True)
    root = 1.0 / jnp.sqrt(diag)
    scaled = full * root
    return jnp.where(c < r, scaled, jnp.where(c == r, root, 0.0))


def factor_kernel(stages, at_ref, a_ref, t_ref):
    n = a_ref.shape[0]
    count = n // IB
    t_ref[...] = a_ref[...]
    block_of = lax.broadcasted_iota(jnp.int32, (IB, n), 1) // IB
    begin = at_ref[0]

    def stage(step, carry):
        p = begin + step
        at = pl.ds(pl.multiple_of(p * IB, IB), IB)
        w = eliminate(t_ref[at, at])
        pre = t_ref[at, :]
        done = jnp.dot(w, pre, precision=HIGHEST, preferred_element_type=jnp.float32)
        t_ref[at, :] = done
        t_ref[at, at] = w
        fresh = t_ref[at, :]

        def row(i, inner):
            to = pl.ds(pl.multiple_of(i * IB, IB), IB)
            lower = t_ref[at, to]
            delta = lax.dot_general(
                lower, fresh, (((0,), (0,)), ((), ())),
                precision=HIGHEST, preferred_element_type=jnp.float32,
            )
            t_ref[to, :] = jnp.where(block_of == p, 0.0, t_ref[to, :]) - delta
            return inner

        lax.fori_loop(p + 1, count, row, 0)
        return carry

    lax.fori_loop(0, stages, stage, 0)


def factor_part(square, begin, stages):
    n = square.shape[0]
    return pl.pallas_call(
        functools.partial(factor_kernel, stages),
        out_shape=jax.ShapeDtypeStruct((n, n), jnp.float32),
        in_specs=[
            pl.BlockSpec(memory_space=pltpu.SMEM),
            pl.BlockSpec(memory_space=pltpu.VMEM),
        ],
        out_specs=pl.BlockSpec(memory_space=pltpu.VMEM),
        compiler_params=pltpu.CompilerParams(vmem_limit_bytes=24 * 1024 * 1024),
        cost_estimate=pl.CostEstimate(
            flops=15_000_000_000 * stages // 2, bytes_accessed=2 * n * n * 4, transcendentals=0
        ),
        name="factor",
    )(jnp.full((1,), begin, jnp.int32), square)


def split(x):
    hi = x.astype(jnp.bfloat16)
    lo = (x - hi.astype(jnp.float32)).astype(jnp.bfloat16)
    return hi, lo


def rows_kernel(x_ref, y_ref, w_ref, p_ref, h_ref, l_ref):
    b = x_ref.shape[1]
    dot = functools.partial(
        lax.dot_general, dimension_numbers=(((1,), (1,)), ((), ())),
        precision=HIGHEST, preferred_element_type=jnp.float32,
    )
    x, y = x_ref[0], y_ref[0]
    first = dot(x, w_ref[:b, :b])
    second = dot(x, w_ref[b:, :b]) + dot(y, w_ref[b:, b:])
    for at, value in ((0, first), (b, second)):
        hi, lo = split(value)
        p_ref[0, :, at : at + b] = value
        h_ref[0, :, at : at + b] = hi
        l_ref[0, :, at : at + b] = lo


def cols_kernel(x_ref, y_ref, w_ref, h_ref, l_ref):
    b = x_ref.shape[1]
    dot = functools.partial(
        jnp.dot, precision=HIGHEST, preferred_element_type=jnp.float32
    )
    x, y = x_ref[0], y_ref[0]
    first = dot(w_ref[:b, :b], x)
    second = dot(w_ref[b:, :b], x) + dot(w_ref[b:, b:], y)
    for at, value in ((0, first), (b, second)):
        hi, lo = split(value)
        h_ref[0, at : at + b, :] = hi
        l_ref[0, at : at + b, :] = lo


def solve(kernel, x, y, w, shapes, name):
    m, b, _ = x.shape
    tile = pl.BlockSpec((1, b, b), lambda i: (i, 0, 0))
    return pl.pallas_call(
        kernel,
        out_shape=[jax.ShapeDtypeStruct((m, *shape), dtype) for shape, dtype in shapes],
        grid=(m,),
        in_specs=[tile, tile, pl.BlockSpec(memory_space=pltpu.VMEM)],
        out_specs=[pl.BlockSpec((1, *shape), lambda i: (i, 0, 0)) for shape, _ in shapes],
        compiler_params=pltpu.CompilerParams(vmem_limit_bytes=44 * 1024 * 1024),
        cost_estimate=pl.CostEstimate(
            flops=m * 36 * b**3, bytes_accessed=m * b * b * 24, transcendentals=0
        ),
        name=name,
    )(x, y, w)


def update_kernel(n_row, n_col, at_ref, a_ref, ph_ref, pl_ref, qh_ref, ql_ref, new_ref, o_ref):
    i, j = pl.program_id(0), pl.program_id(1)
    t = i * n_row + at_ref[0]
    s = j * n_col + at_ref[1]

    @pl.when(t < s)
    def _():
        o_ref[...] = jnp.zeros_like(o_ref)

    @pl.when((t >= s) & (s < STEPS))
    def _():
        o_ref[...] = new_ref[...].reshape(o_ref.shape)

    @pl.when((t >= s) & (s >= STEPS))
    def _():
        dot = functools.partial(jnp.dot, preferred_element_type=jnp.float32)
        qh, ql = qh_ref[j], ql_ref[j]
        ph, plo = ph_ref[0], pl_ref[0]
        acc = dot(ph, qh) + (dot(ph, ql) + dot(plo, qh))
        o_ref[...] = a_ref[...] - acc.reshape(o_ref.shape)


def update(trailing, place, panel, across, new_column, n_row, n_col):
    rows, _, b, cols, _, _ = trailing.shape
    ph, plo = panel
    qh, ql = across
    depth = ph.shape[-1]

    def needed(i, j, at):
        last = jnp.maximum((i * n_row + at[0] - at[1]) // n_col, 0)
        return jnp.minimum(j, jnp.minimum(last, cols - 1))

    tile = (1, 1, b, 1, 1, b)
    whole = pl.BlockSpec(memory_space=pltpu.VMEM)
    return pl.pallas_call(
        functools.partial(update_kernel, n_row, n_col),
        out_shape=jax.ShapeDtypeStruct(trailing.shape, jnp.float32),
        grid_spec=pltpu.PrefetchScalarGridSpec(
            num_scalar_prefetch=1,
            grid=(rows, cols),
            in_specs=[
                pl.BlockSpec(tile, lambda i, j, at: (i, 0, 0, needed(i, j, at), 0, 0)),
                pl.BlockSpec((1, b, depth), lambda i, j, at: (i, 0, 0)),
                pl.BlockSpec((1, b, depth), lambda i, j, at: (i, 0, 0)),
                whole,
                whole,
                pl.BlockSpec((1, b, b), lambda i, j, at: (i, 0, 0)),
            ],
            out_specs=pl.BlockSpec(tile, lambda i, j, at: (i, 0, 0, j, 0, 0)),
        ),
        compiler_params=pltpu.CompilerParams(vmem_limit_bytes=48 * 1024 * 1024),
        name="update",
    )(place, trailing, ph, plo, qh, ql, new_column)


def corner_square(seed):
    a00, a10, a11 = seed
    return jnp.block([[a00, a10.T], [a10, a11]])


def local(trailing):
    row_tiles, _, b, col_tiles, _, _ = trailing.shape
    n_row = lax.axis_size("row")
    n_col = lax.axis_size("col")
    r = lax.axis_index("row")
    c = lax.axis_index("col")
    own = trailing[:, 0, :, 0, 0, :]
    corner = own[0]
    seed = [
        jnp.where((r == t) & (c == s), corner, 0.0) for t, s in ((0, 0), (1, 0), (1, 1))
    ]
    seed = lax.psum(jnp.stack(seed), ("row", "col"))

    z = r // 2
    hops = n_row // 2 - 1
    steps = col_tiles + hops - 1
    tiles = [trailing[0, 0, :, j, 0, :] for j in range(col_tiles)]
    arrived = tiles[0]
    parts = 4
    per = 2 * b // IB // parts
    gate = min(3, steps)
    square = None
    work = 0
    held = own
    keep = {}
    for step in range(steps):
        if step == gate:
            arrived, seed, own_late = lax.optimization_barrier((arrived, seed, own))
            square = corner_square(seed)
            held = own_late
        elif step > gate and work < parts:
            arrived, square = lax.optimization_barrier((arrived, square))
        head = tiles[step] if step < col_tiles else tiles[-1]
        send = jnp.where(z == 0, head, arrived)
        arrived = lax.ppermute(send, "row", [(x, x + 2) for x in range(n_row - 2)])
        keep[step] = arrived
        if step >= gate and work < parts:
            square = factor_part(square, work * per, per)
            work += 1
    if square is None:
        square = corner_square(seed)
    while work < parts:
        square = factor_part(square, work * per, per)
        work += 1
    columns = []
    for j in range(col_tiles):
        tile = tiles[j]
        for hop in range(1, hops + 1):
            tile = jnp.where(z == hop, keep[j + hop - 1], tile)
        columns.append(tile)
    columns = jnp.stack(columns)
    swapped = lax.ppermute(columns, "row", [(x, x ^ 1) for x in range(n_row)])
    first_row = r % 2 == 0
    top = jnp.where(first_row, columns, swapped)
    bottom = jnp.where(first_row, swapped, columns)

    d = 2
    while d < n_col:
        more = lax.ppermute(held, "col", [(x, x + d) for x in range(d)])
        held = jnp.where((c >= d) & (c < 2 * d), more, held)
        d *= 2
    other = lax.ppermute(held, "col", [(x, x ^ 1) for x in range(n_col)])
    even = c % 2 == 0
    left = jnp.where(even, held, other)
    right = jnp.where(even, other, held)

    block = jnp.arange(2 * b) // IB
    w = jnp.where(block[:, None] >= block[None, :], square, 0.0)
    f32, bf16 = jnp.float32, jnp.bfloat16
    wide, tall = (b, 2 * b), (2 * b, b)
    panel, *halves = solve(
        rows_kernel, left, right, w, [(wide, f32), (wide, bf16), (wide, bf16)], "rows"
    )
    across = solve(cols_kernel, top, bottom, w, [(tall, bf16), (tall, bf16)], "cols")
    mine_col = jnp.where(c == 0, panel[:, :, :b], panel[:, :, b:])
    rows_at = jnp.arange(row_tiles, dtype=jnp.int32) * n_row + r
    new_column = jnp.where((rows_at == c)[:, None, None], jnp.tril(mine_col), mine_col)
    place = jnp.stack([r, c]).astype(jnp.int32)
    return update(trailing, place, halves, across, new_column, n_row, n_col)


def solution(mesh):
    spec = P(None, "row", None, None, "col", None)
    return jax.shard_map(local, mesh=mesh, in_specs=(spec,), out_specs=spec, check_vma=False)
```
